512 devices in a mesh: blk: 32 (over y, x_lo, core), col: 16 (over x_hi, z).
Axes of the slice: x: 4 (x_hi: 2, x_lo: 2; x = x_hi * 2 + x_lo), y: 8, z: 8, core: 2. Of those that a mesh axis runs over, the one named last changes fastest.
Arguments:
- features: bfloat16 [65536, 768], P(('blk', 'col')), may hold values from -24 to 24
- node_order: int32 [512, 128], P(('blk', 'col')), may hold values from 0 to 127, each once within a row
- weight: bfloat16 [768, 256], replicated, may hold values from -0.21875 to 0.21875
- cotangent: bfloat16 [65536, 256], P(('blk', 'col')), may hold values from -6 to 6
- tile_list: int32 [49152, 2], P(('blk', 'col')), may hold values from -1 to 511, as said below
- tile_values: bfloat16 [49152, 128, 128], P(('blk', 'col')), may hold values from -0.078125 to 0.078125
Outputs:
- hidden: bfloat16 [65536, 256], P(('blk', 'col'))
- x_grad: bfloat16 [65536, 768], P(('blk', 'col'))
- weight_grad: float32 [768, 256], replicated
The draws below stay inside these ranges and needn't reach their ends.
Inputs may be any that keep to these rules, and one draw needn't show every extreme that they name: `tile_list`: slots held by one device come in groups of 3, group g taking tiles whose column block is among the 1 block that device (blk index g, the holder's col index) holds. A live slot's row block is among the 16 blocks of the holder's blk index; an empty slot has row block -1 and a valid column block. Every device has at least one full group.
All inputs are finite; a program needn't handle non-finite values.
Results may differ from the reference program's by a relative error of at most 0.0075.
Values may be sent and summed in bfloat16 or wider, within the bound.
No kernel may reach another device: no remote copies, remote signals or barrier semaphores. Data moves between devices by JAX's collectives and lax.ppermute only.
A program may use at most 128 MiB of HBM per device.

```python
import jax
import jax.numpy as jnp
from jax import lax

FIN = 768
HID = 256
TILE = 128
SLOTS = 3
CB = 1
RB = 16
NB = 512
NODES = 65536
TILES = 49152
N_BLK = 32
N_COL = 16


def draw_tile_list(key, part):
    key = jax.random.fold_in(key, 11)
    keys = jax.random.split(key, 4)
    devices = N_BLK * N_COL
    level = jax.random.randint(keys[0], (devices, 1), 1, SLOTS + 1)
    raw_count = jax.random.randint(keys[1], (devices, N_BLK), 0, SLOTS + 1)
    live_count = jnp.minimum(raw_count, level)
    device_ids = jnp.arange(devices, dtype=jnp.int32)[:, None]
    group_ids = jnp.arange(N_BLK, dtype=jnp.int32)[None, :]
    live_count = jnp.where(group_ids == device_ids % N_BLK, SLOTS, live_count)
    slot_ids = jnp.arange(SLOTS, dtype=jnp.int32)
    live = slot_ids[None, None, :] < live_count[:, :, None]
    blk_of = device_ids // N_COL
    col_of = device_ids % N_COL
    row_pick = jax.random.randint(keys[2], (devices, N_BLK, SLOTS), 0, RB)
    col_pick = jax.random.randint(keys[3], (devices, N_BLK, SLOTS), 0, CB)
    row_block = blk_of[:, :, None] * RB + row_pick
    col_block = group_ids[:, :, None] * RB + col_of[:, :, None] * CB + col_pick
    row_block = jnp.where(live, row_block, -1)
    return jnp.stack([row_block.reshape(-1), col_block.reshape(-1)], axis=1).astype(jnp.int32)


def strengthened(drawn, own_key, source, target, blocks, factor):
    def block_of(dim):
        return (jnp.arange(drawn.shape[dim]) // (drawn.shape[dim] // blocks)).reshape((-1,) + (1,) * (drawn.ndim - 1 - dim))

    near = jax.random.permutation(own_key, blocks)[block_of(target)]
    second = (block_of(target) + blocks // 2) % blocks
    return jnp.where((block_of(source) == near) | (block_of(source) == second), factor * drawn, drawn)


def block_scale(stream_key, shape, pieces, least, top_value):
    gain, own = 1.0, jax.random.fold_in(stream_key, 6)
    for dim, parts in pieces:
        heights = jnp.exp(jax.random.uniform(jax.random.fold_in(own, dim), (parts,), jnp.float32, least / len(pieces), top_value / len(pieces)))
        gain = gain * jnp.repeat(heights, shape[dim] // parts).reshape([-1 if axis == dim else 1 for axis in range(len(shape))])
    return gain


def normal_values(stream_key, dims, width, reach, shards=(), kind=jnp.bfloat16):
    entries = width * jax.random.normal(stream_key, dims, jnp.float32)
    if shards:
        entries = entries * block_scale(stream_key, dims, shards, -0.22, 0.18)
    return jnp.clip(entries, -reach, reach).astype(kind)


def heavy_noise(key, shape, deviation, most, shards, heavy, kind=jnp.bfloat16):
    result = deviation * jax.random.normal(key, shape, jnp.float32)
    if shards:
        result = result * block_scale(key, shape, shards, -0.22, 0.18)
    return jnp.clip(strengthened(result, jax.random.fold_in(key, 3), *heavy), -most, most).astype(kind)


def setup_inputs(seed: int = 0) -> dict:
    splits = jax.random.split(jax.random.key(seed), 7)
    features = heavy_noise(splits[0], (NODES, FIN), 1.0, 24.0, ((0, 512),), (0, 1, 256, 6.0))
    node_order = jax.vmap(lambda own: jax.random.permutation(own, TILE))(jax.random.split(splits[1], NB)).reshape((NB, TILE)).astype(jnp.int32)
    weight = normal_values(splits[2], (FIN, HID), FIN ** -0.5, 0.21875)
    cotangent = normal_values(splits[3], (NODES, HID), 1.0, 6.0, ((0, 512),))
    tile_list = draw_tile_list(jax.random.fold_in(splits[6], 71), 0)
    tile_values = normal_values(splits[5], (TILES, TILE, TILE), (TILE * SLOTS * N_BLK // (2 * CB)) ** -0.5, 0.078125, ((0, 512),))
    return dict(features=features, node_order=node_order, weight=weight, cotangent=cotangent, tile_list=tile_list, tile_values=tile_values)


def gelu_tanh(values):
    return jax.nn.gelu(values, approximate=True)

def reference(features, node_order, weight, cotangent, tile_list, tile_values):
    blocks3 = features.reshape(NB, TILE, FIN)
    reordered = jnp.take_along_axis(blocks3, node_order[:, :, None], axis=1).reshape(NODES, FIN)
    panel = jnp.dot(reordered, weight, preferred_element_type=jnp.float32).astype(jnp.bfloat16)
    row_ids = tile_list[:, 0]
    col_ids = tile_list[:, 1]
    safe_rows = jnp.where(row_ids >= 0, row_ids, NB).astype(jnp.int32)
    per_dev = SLOTS * N_BLK
    group_rows = safe_rows.reshape(N_BLK * N_COL, per_dev)
    group_cols = col_ids.reshape(N_BLK * N_COL, per_dev)
    group_tiles = tile_values.reshape(N_BLK * N_COL, per_dev, TILE, TILE)
    panel3 = panel.reshape(NB, TILE, HID)

    def forward_step(total, item):
        tiles_now, rows_now, cols_now = item
        picked = panel3[cols_now].astype(jnp.float32)
        product = jnp.einsum('sij,sjf->sif', tiles_now.astype(jnp.float32), picked)
        return (total.at[rows_now].add(product), None)
    start_fwd = jnp.zeros((NB + 1, TILE, HID), jnp.float32)
    total_fwd, _ = lax.scan(forward_step, start_fwd, (group_tiles, group_rows, group_cols))
    agg = total_fwd[:NB].reshape(NODES, HID)
    hidden = gelu_tanh(agg).astype(jnp.bfloat16)
    _, pull = jax.vjp(gelu_tanh, agg)
    agg_grad = pull(cotangent.astype(jnp.float32))[0].astype(jnp.bfloat16)
    grad_pad = jnp.concatenate([agg_grad.reshape(NB, TILE, HID), jnp.zeros((1, TILE, HID), jnp.bfloat16)], axis=0)

    def backward_step(total, item):
        tiles_now, rows_now, cols_now = item
        picked = grad_pad[rows_now].astype(jnp.float32)
        product = jnp.einsum('sij,sif->sjf', tiles_now.astype(jnp.float32), picked)
        return (total.at[cols_now].add(product), None)
    start_bwd = jnp.zeros((NB, TILE, HID), jnp.float32)
    total_bwd, _ = lax.scan(backward_step, start_bwd, (group_tiles, group_rows, group_cols))
    panel_grad = total_bwd.reshape(NODES, HID).astype(jnp.bfloat16)
    weight_grad = jnp.dot(reordered.T, panel_grad, preferred_element_type=jnp.float32) * NODES ** (-0.5)
    row_grad = jnp.dot(panel_grad, weight.T, preferred_element_type=jnp.float32).astype(jnp.bfloat16)
    placed = jnp.zeros((NB, TILE, FIN), jnp.bfloat16)
    block_ids = jnp.arange(NB, dtype=jnp.int32)[:, None]
    placed = placed.at[block_ids, node_order].set(row_grad.reshape(NB, TILE, FIN))
    x_grad = placed.reshape(NODES, FIN)
    return (hidden, x_grad, weight_grad)
```

```python
import functools

import jax
import jax.numpy as jnp
from jax import lax
from jax.experimental import pallas as pl
from jax.experimental.pallas import tpu as pltpu
from jax.sharding import Mesh
from jax.sharding import PartitionSpec as P

AXES = ("y", "xl", "core", "xh", "z")
CHIPS = ("y", "xl")
COLS = ("xh", "z")
SWAP = [(0, 1), (1, 0)]
VMEM = pl.BlockSpec(memory_space=pltpu.VMEM)
SMEM = pl.BlockSpec(memory_space=pltpu.SMEM)
F32 = jnp.float32
BF16 = jnp.bfloat16


def swap(value):
    return lax.ppermute(value, "core", SWAP)


def exchange(value, axes):
    return lax.all_to_all(value, axes, 0, 0, tiled=True)


def params(mib):
    return pltpu.CompilerParams(vmem_limit_bytes=mib * 1024 * 1024)


def dot(a, b, contract):
    return lax.dot_general(a, b, (contract, ((), ())), preferred_element_type=F32)


def source_onehot(order):
    size = order.shape[1]
    rows = lax.broadcasted_iota(jnp.int32, (size, size), 0)
    return (rows == order).astype(F32).astype(BF16)


def panel_kernel(core, order, features, weight, mine, theirs):
    half = mine.shape[1]
    whole = dot(features[...], weight[...], ((1,), (0,))).astype(BF16)
    whole = dot(source_onehot(order[...]), whole, ((0,), (0,))).astype(BF16)
    left, right = whole[:, :half], whole[:, half:]
    first = core[0] == 0
    mine[...] = jnp.where(first, left, right)
    theirs[...] = jnp.where(first, right, left)


def forward_kernel(core, rows_own, rows_other, panels, own, other, out, total):
    chips = panels.shape[0]
    size = panels.shape[2]
    ranges = out.shape[0]
    slots = own.shape[0] // (2 * chips)
    total[...] = jnp.zeros_like(total)
    me = core[0]

    def one_chip(chip, carry):
        for bit in range(2):
            group = 2 * chip + bit
            panel = panels[chip, bit ^ me]
            for which, (tiles, rows) in enumerate(((own, rows_own), (other, rows_other))):
                stack = tiles[pl.ds(group * slots, slots)].reshape(slots * size, size)
                product = dot(stack, panel, ((1,), (0,)))
                for slot in range(slots):
                    row = rows[group * slots + slot]
                    place = which * (ranges + 1) + row
                    total[place] += product[slot * size:(slot + 1) * size]
        return carry

    lax.fori_loop(0, chips, one_chip, 0)
    for which in range(2):
        base = which * (ranges + 1)
        out[:, which] = total[base:base + ranges].astype(BF16)


def middle_kernel(parts, cotangent, hidden, grad):
    scale = (2.0 / jnp.pi) ** 0.5
    for which in range(2):
        agg = jnp.sum(parts[:, which].astype(F32), axis=0)
        square = agg * agg
        slope = scale * (1.0 + 3.0 * 0.044715 * square)
        bend = jnp.tanh(scale * (agg + 0.044715 * (agg * square)))
        cdf = 0.5 * (1.0 + bend)
        hidden[which] = (agg * cdf).astype(BF16)
        upstream = cotangent[which].astype(F32)
        derivative = cdf + agg * (0.5 * (1.0 - bend * bend) * slope)
        turned = (upstream * derivative).T.astype(BF16)
        grad[:, which] = jnp.broadcast_to(turned[None], (grad.shape[0],) + turned.shape)


def backward_kernel(core, rows_own, rows_other, grads, own, other, out):
    chips = out.shape[0]
    size = grads.shape[2]
    ranges = grads.shape[0]
    slots = own.shape[0] // (2 * chips)
    me = core[0]

    def one_chip(chip, carry):
        for bit in range(2):
            group = 2 * chip + bit
            lefts = []
            rights = []
            for which, (tiles, rows) in enumerate(((own, rows_own), (other, rows_other))):
                for slot in range(slots):
                    row = rows[group * slots + slot]
                    block = grads[jnp.minimum(row, ranges - 1), which]
                    lefts.append(jnp.where(row < ranges, block, jnp.zeros_like(block)))
                rights.append(tiles[pl.ds(group * slots, slots)].reshape(slots * size, size))
            left = jnp.concatenate(lefts, axis=1)
            right = jnp.concatenate(rights, axis=0)
            out[chip, bit ^ me] = dot(left, right, ((1,), (0,))).astype(BF16)
        return carry

    lax.fori_loop(0, chips, one_chip, 0)


def weight_kernel(scale, parts, order_own, order_other, own, other, turned, term):
    total = 0.0
    for which, (order, features) in enumerate(((order_own, own), (order_other, other))):
        panel_grad = jnp.sum(parts[:, which].astype(F32), axis=0).astype(BF16)
        placed = dot(panel_grad, source_onehot(order[...]), ((1,), (1,))).astype(BF16)
        turned[which] = placed
        total = total + dot(placed, features[...], ((1,), (0,)))
    term[...] = (total * scale).T.astype(BF16)


def feature_kernel(core, mine, theirs, weight, out):
    half = mine.shape[0]
    me = core[0]
    near = weight[:, pl.ds(pl.multiple_of(me * half, half), half)]
    far = weight[:, pl.ds(pl.multiple_of((1 - me) * half, half), half)]
    total = dot(mine[...], near, ((0,), (1,))) + dot(theirs[...], far, ((0,), (1,)))
    out[...] = total.astype(BF16)


def per_device(features, node_order, weight, cotangent, tile_list, tile_values):
    tiles, size, _ = tile_values.shape
    in_width, hid = weight.shape
    half = hid // 2
    chips = lax.axis_size("y") * lax.axis_size("xl")
    ranges = lax.axis_size("xh") * lax.axis_size("z")
    nodes = 2 * chips * ranges * size
    core = lax.axis_index("core").astype(jnp.int32).reshape(1)
    first = core[0] == 0

    def halves(value):
        left, right = value[:, :half], value[:, half:]
        return jnp.where(first, left, right), jnp.where(first, right, left)

    def joined(near, far):
        return jnp.where(
            first, jnp.concatenate([near, far], 1), jnp.concatenate([far, near], 1)
        )

    mine, theirs = pl.pallas_call(
        panel_kernel,
        out_shape=[jax.ShapeDtypeStruct((size, half), BF16)] * 2,
        in_specs=[SMEM, VMEM, VMEM, VMEM],
        out_specs=[VMEM] * 2,
        compiler_params=params(16),
    )(core, node_order, features, weight)
    pair = jnp.stack([mine, swap(theirs)])
    panels = exchange(jnp.broadcast_to(pair[None], (chips, 2, size, half)), CHIPS)

    row_ids = tile_list[:, 0]
    rows_own = jnp.where(row_ids >= 0, row_ids % ranges, ranges)
    rows_other = swap(rows_own)
    tiles_other = swap(tile_values)
    order_other = swap(node_order)
    features_other = swap(features)
    near_cot, far_cot = halves(cotangent)
    cot_pair = jnp.stack([near_cot, swap(far_cot)])

    partial = pl.pallas_call(
        forward_kernel,
        out_shape=jax.ShapeDtypeStruct((ranges, 2, size, half), BF16),
        in_specs=[SMEM, SMEM, SMEM, VMEM, VMEM, VMEM],
        out_specs=VMEM,
        scratch_shapes=[pltpu.VMEM((2 * (ranges + 1), size, half), F32)],
        compiler_params=params(24),
    )(core, rows_own, rows_other, panels, tile_values, tiles_other)
    parts = exchange(partial, COLS)
    hidden_pair, grad = pl.pallas_call(
        middle_kernel,
        out_shape=[
            jax.ShapeDtypeStruct((2, size, half), BF16),
            jax.ShapeDtypeStruct((ranges, 2, half, size), BF16),
        ],
        in_specs=[VMEM] * 2,
        out_specs=[VMEM] * 2,
        compiler_params=params(16),
    )(parts, cot_pair)
    grads = exchange(grad, COLS)
    hidden = joined(hidden_pair[0], swap(hidden_pair[1]))

    contribution = pl.pallas_call(
        backward_kernel,
        out_shape=jax.ShapeDtypeStruct((chips, 2, half, size), BF16),
        in_specs=[SMEM, SMEM, SMEM, VMEM, VMEM, VMEM],
        out_specs=VMEM,
        compiler_params=params(24),
    )(core, rows_own, rows_other, grads, tile_values, tiles_other)
    parts = exchange(contribution, CHIPS)
    turned, term = pl.pallas_call(
        functools.partial(weight_kernel, nodes ** -0.5),
        out_shape=[
            jax.ShapeDtypeStruct((2, half, size), BF16),
            jax.ShapeDtypeStruct((in_width, half), BF16),
        ],
        in_specs=[VMEM] * 5,
        out_specs=[VMEM] * 2,
        compiler_params=params(16),
    )(parts, node_order, order_other, features, features_other)

    def summed(value):
        return jnp.sum(value.astype(F32), axis=0).astype(BF16)

    share = in_width // ranges
    term = summed(exchange(term.reshape(ranges, share, half), COLS))
    term = summed(exchange(jnp.broadcast_to(term[None], (chips, share, half)), CHIPS))
    term = exchange(jnp.broadcast_to(term[None], (ranges, share, half)), COLS)
    term = term.reshape(in_width, half)
    weight_grad = joined(term, swap(term)).astype(F32)

    x_grad = pl.pallas_call(
        feature_kernel,
        out_shape=jax.ShapeDtypeStruct((size, in_width), BF16),
        in_specs=[SMEM, VMEM, VMEM, VMEM],
        out_specs=VMEM,
        compiler_params=params(16),
    )(core, turned[0], swap(turned[1]), weight)
    return (hidden, x_grad, weight_grad)


def solution(mesh):
    blk, col = mesh.devices.shape
    fine = Mesh(mesh.devices.reshape(blk // 4, 2, 2, 2, col // 2), AXES)
    rows = P(AXES)
    return jax.shard_map(
        per_device,
        mesh=fine,
        in_specs=(rows, rows, P(), rows, rows, rows),
        out_specs=(rows, rows, P()),
        check_vma=False,
    )
```

```python
import functools

import jax
import jax.numpy as jnp
from jax import lax
from jax.experimental import pallas as pl
from jax.experimental.pallas import tpu as pltpu
from jax.sharding import Mesh
from jax.sharding import PartitionSpec as P

AXES = ("y", "xl", "core", "xh", "z")
CHIPS = ("y", "xl")
COLS = ("xh", "z")
SWAP = [(0, 1), (1, 0)]
VMEM = pl.BlockSpec(memory_space=pltpu.VMEM)
SMEM = pl.BlockSpec(memory_space=pltpu.SMEM)
ANY = pl.BlockSpec(memory_space=pl.ANY)
DMA = pltpu.SemaphoreType.DMA
F32 = jnp.float32
BF16 = jnp.bfloat16


def swap(value):
    return lax.ppermute(value, "core", SWAP)


def exchange(value, axes):
    return lax.all_to_all(value, axes, 0, 0, tiled=True)


def copies_kernel(near, far, out):
    for which, half in enumerate((near, far)):
        out[:, which] = jnp.broadcast_to(half[...][None], (out.shape[0],) + half.shape)


def gathered_panels(mine, received, held, first, count):
    shape = (count, 2) + mine.shape

    def gather(near, far):
        copies = pl.pallas_call(
            copies_kernel,
            out_shape=jax.ShapeDtypeStruct(shape, near.dtype),
            in_specs=[VMEM] * 2,
            out_specs=VMEM,
            compiler_params=params(16),
        )(near, far)
        return exchange(copies, "y")

    def skip(near, far):
        return jnp.zeros(shape, near.dtype)

    panels = lax.cond(first, gather, skip, mine, received)
    panels, held = lax.optimization_barrier((panels, held))
    held = lax.ppermute(held, "core", [(0, 1)])
    panels = lax.cond(first, lambda near, far, done: done,
                      lambda near, far, done: gather(near, far), mine, held, panels)
    return panels, lax.ppermute(panels, "xl", SWAP)


def in_hbm(value):
    return pltpu.with_memory_space_constraint(value, pltpu.HBM)


def params(mib):
    return pltpu.CompilerParams(vmem_limit_bytes=mib * 1024 * 1024)


def dot(a, b, contract):
    return lax.dot_general(a, b, (contract, ((), ())), preferred_element_type=F32)


def source_onehot(order):
    size = order.shape[1]
    rows = lax.broadcasted_iota(jnp.int32, (size, size), 0)
    return (rows == order).astype(F32).astype(BF16)


def panel_kernel(ranges, core, order_in, rows_in, features, weight_in, cotangent,
                 mine, near_cot, pack, places, order, rows, weight, sem):
    size, half = mine.shape
    hid = 2 * half
    me = core[0]
    near = pl.ds(pl.multiple_of(me * half, half), half)
    far = pl.ds(pl.multiple_of((1 - me) * half, half), half)
    copies = [
        pltpu.make_async_copy(source, target, sem.at[index])
        for index, (source, target) in enumerate((
            (weight_in, weight),
            (features, pack.at[:size, hid:]),
            (order_in, order),
            (rows_in, rows),
            (cotangent.at[:, near], near_cot),
            (cotangent.at[:, far], pack.at[:size, half:hid]),
        ))
    ]
    for copy in copies:
        copy.start()
    for copy in copies:
        copy.wait()
    whole = dot(pack[:size, hid:], weight[...], ((1,), (0,))).astype(BF16)
    whole = dot(source_onehot(order[...]), whole, ((0,), (0,))).astype(BF16)
    first = me == 0
    left, right = whole[:, :half], whole[:, half:hid]
    mine[...] = jnp.where(first, left, right)
    pack[:size, :half] = jnp.where(first, right, left)
    extra = pack.shape[0] - size
    pack[size:, :] = jnp.zeros((extra, pack.shape[1]), BF16)
    numbers = (extra, size)
    pack[size:, :size] = jnp.broadcast_to(order[...].astype(F32), numbers).astype(BF16)
    ids = rows[:1]
    place = jnp.where(ids >= 0, lax.rem(ids, ranges), ranges)
    places[...] = place
    numbers = (extra, place.shape[1])
    place = jnp.broadcast_to(place.astype(F32), numbers).astype(BF16)
    pack[size:, size:size + place.shape[1]] = place


CHUNKS = 4


def forward_kernel(core_x, rows_own, rows_other, near_in, far_in, own, other_in, out,
                   near, far, other, total_own, total_other, sem):
    across, _, size, _ = near.shape
    ranges = out.shape[0]
    slots = own.shape[0] // (4 * across)
    me, x = core_x[0], core_x[1]
    part = other.shape[0] // CHUNKS
    arriving = [
        pltpu.make_async_copy(near_in, near, sem.at[CHUNKS]),
        pltpu.make_async_copy(far_in, far, sem.at[CHUNKS + 1]),
    ]
    for chunk in range(CHUNKS):
        tiles = pl.ds(chunk * part, part)
        arriving.append(
            pltpu.make_async_copy(other_in.at[tiles], other.at[tiles], sem.at[chunk]))
    for copy in arriving:
        copy.start()
    total_own[...] = jnp.zeros_like(total_own)
    total_other[...] = jnp.zeros_like(total_other)
    for copy in arriving:
        copy.wait()
    for panels, column in ((near, x), (far, 1 - x)):
        for y in range(across):
            for bit in range(2):
                panel = panels[y, bit ^ me]
                base = ((2 * y + column) * 2 + bit) * slots
                here = pl.ds(base, slots)
                ours = dot(own[here].reshape(slots * size, size), panel, ((1,), (0,)))
                theirs = dot(other[here].reshape(slots * size, size), panel, ((1,), (0,)))
                for slot in range(slots):
                    take = slice(slot * size, (slot + 1) * size)
                    total_own[rows_own[0, base + slot]] += ours[take]
                    total_other[rows_other[0, base + slot]] += theirs[take]
    for which, total in enumerate((total_own, total_other)):
        out[:, which] = total[:ranges].astype(BF16)


def middle_kernel(parts, near_cot, pack, hidden, grad):
    size, half = near_cot.shape
    scale = (2.0 / jnp.pi) ** 0.5
    for which in range(2):
        agg = jnp.sum(parts[:, which].astype(F32), axis=0)
        square = agg * agg
        slope = scale * (1.0 + 3.0 * 0.044715 * square)
        bend = jnp.tanh(scale * (agg + 0.044715 * (agg * square)))
        cdf = 0.5 * (1.0 + bend)
        hidden[which] = (agg * cdf).astype(BF16)
        upstream = near_cot[...] if which == 0 else pack[:size, half:2 * half]
        derivative = cdf + agg * (0.5 * (1.0 - bend * bend) * slope)
        turned = (upstream.astype(F32) * derivative).T.astype(BF16)
        grad[:, which] = jnp.broadcast_to(turned[None], (grad.shape[0],) + turned.shape)


def backward_kernel(core, rows_own, rows_other, grads, own, other_in, out, other, sem):
    chips = out.shape[0]
    ranges, _, _, size = grads.shape
    slots = own.shape[0] // (2 * chips)
    part = chips // CHUNKS
    me = core[0]
    arriving = []
    for chunk in range(CHUNKS):
        tiles = pl.ds(chunk * part * 2 * slots, part * 2 * slots)
        arriving.append(
            pltpu.make_async_copy(other_in.at[tiles], other.at[tiles], sem.at[chunk]))
        arriving[-1].start()
    for chunk in range(CHUNKS):
        arriving[chunk].wait()
        for group in range(2 * part * chunk, 2 * part * (chunk + 1)):
            lefts = []
            rights = []
            for which, (tiles, rows) in enumerate(((own, rows_own), (other, rows_other))):
                for slot in range(group * slots, (group + 1) * slots):
                    row = rows[0, slot]
                    block = grads[jnp.minimum(row, ranges - 1), which]
                    lefts.append(jnp.where(row < ranges, block, jnp.zeros_like(block)))
                here = slice(group * slots, (group + 1) * slots)
                rights.append(tiles[here].reshape(slots * size, size))
            left = jnp.concatenate(lefts, axis=1)
            right = jnp.concatenate(rights, axis=0)
            out[group // 2, (group % 2) ^ me] = dot(left, right, ((1,), (0,))).astype(BF16)


def weight_kernel(scale, parts, order, features, pack, turned, term):
    size = features.shape[0]
    hid = pack.shape[1] - features.shape[1]
    order_other = pack[size:, :size][:1].astype(F32).astype(jnp.int32)
    both = ((order[...], features[...]), (order_other, pack[:size, hid:]))
    total = 0.0
    for which, (source, values) in enumerate(both):
        panel_grad = jnp.sum(parts[:, which].astype(F32), axis=0).astype(BF16)
        placed = dot(panel_grad, source_onehot(source), ((1,), (1,))).astype(BF16)
        turned[which] = placed
        total = total + dot(placed, values, ((1,), (0,)))
    term[...] = (total * scale).T.astype(BF16)


def feature_kernel(core, mine, theirs, weight, out):
    half = mine.shape[0]
    me = core[0]
    near = weight[:, pl.ds(pl.multiple_of(me * half, half), half)]
    far = weight[:, pl.ds(pl.multiple_of((1 - me) * half, half), half)]
    total = dot(mine[...], near, ((0,), (1,))) + dot(theirs[...], far, ((0,), (1,)))
    out[...] = total.astype(BF16)


def per_device(features, node_order, weight, cotangent, tile_list, tile_values):
    tiles, size, _ = tile_values.shape
    in_width, hid = weight.shape
    half = hid // 2
    chips = lax.axis_size("y") * lax.axis_size("xl")
    ranges = lax.axis_size("xh") * lax.axis_size("z")
    nodes = 2 * chips * ranges * size
    core = lax.axis_index("core").astype(jnp.int32).reshape(1)
    first = core[0] == 0

    def joined(near, far):
        return jnp.where(
            first, jnp.concatenate([near, far], 1), jnp.concatenate([far, near], 1)
        )

    mine, near_cot, pack, rows_own = pl.pallas_call(
        functools.partial(panel_kernel, ranges),
        out_shape=[
            jax.ShapeDtypeStruct((size, half), BF16),
            jax.ShapeDtypeStruct((size, half), BF16),
            jax.ShapeDtypeStruct((size + 16, hid + in_width), BF16),
            jax.ShapeDtypeStruct((1, tiles), jnp.int32),
        ],
        in_specs=[SMEM] + [ANY] * 5,
        out_specs=[VMEM] * 4,
        scratch_shapes=[
            pltpu.VMEM((1, size), jnp.int32),
            pltpu.VMEM((2, tiles), jnp.int32),
            pltpu.VMEM((in_width, hid), BF16),
            DMA((6,)),
        ],
        compiler_params=params(16),
    )(core, *map(in_hbm, (node_order, tile_list.T, features, weight, cotangent)))
    held = pack[:size, :half]
    pack, later_tiles = lax.optimization_barrier((swap(pack), tile_values))
    tiles_other = swap(later_tiles)
    rows_other = pack[size:size + 1, size:size + tiles].astype(jnp.int32)
    across = lax.axis_size("y")
    near, far = gathered_panels(mine, pack[:size, :half], held, first, across)
    core_x = jnp.concatenate([core, lax.axis_index("xl").astype(jnp.int32).reshape(1)])

    partial = pl.pallas_call(
        forward_kernel,
        out_shape=jax.ShapeDtypeStruct((ranges, 2, size, half), BF16),
        in_specs=[SMEM, SMEM, SMEM, ANY, ANY, VMEM, ANY],
        out_specs=VMEM,
        scratch_shapes=[
            pltpu.VMEM((across, 2, size, half), BF16),
            pltpu.VMEM((across, 2, size, half), BF16),
            pltpu.VMEM((tiles, size, size), BF16),
            pltpu.VMEM((ranges + 1, size, half), F32),
            pltpu.VMEM((ranges + 1, size, half), F32),
            DMA((CHUNKS + 2,)),
        ],
        compiler_params=params(24),
    )(core_x, rows_own, rows_other, near, far, tile_values, tiles_other)
    parts = exchange(partial, COLS)
    hidden_pair, grad = pl.pallas_call(
        middle_kernel,
        out_shape=[
            jax.ShapeDtypeStruct((2, size, half), BF16),
            jax.ShapeDtypeStruct((ranges, 2, half, size), BF16),
        ],
        in_specs=[VMEM] * 3,
        out_specs=[VMEM] * 2,
        compiler_params=params(16),
    )(parts, near_cot, pack)
    grads = exchange(grad, COLS)
    contribution = pl.pallas_call(
        backward_kernel,
        out_shape=jax.ShapeDtypeStruct((chips, 2, half, size), BF16),
        in_specs=[SMEM, SMEM, SMEM, VMEM, VMEM, ANY],
        out_specs=VMEM,
        scratch_shapes=[
            pltpu.VMEM((tiles, size, size), BF16),
            DMA((CHUNKS,)),
        ],
        compiler_params=params(24),
    )(core, rows_own, rows_other, grads, tile_values, tiles_other)
    parts = exchange(contribution, CHIPS)
    turned, term = pl.pallas_call(
        functools.partial(weight_kernel, nodes ** -0.5),
        out_shape=[
            jax.ShapeDtypeStruct((2, half, size), BF16),
            jax.ShapeDtypeStruct((in_width, half), BF16),
        ],
        in_specs=[VMEM] * 4,
        out_specs=[VMEM] * 2,
        compiler_params=params(16),
    )(parts, node_order, features, pack)

    def summed(value):
        return jnp.sum(value.astype(F32), axis=0).astype(BF16)

    share = in_width // ranges
    term = summed(exchange(term.reshape(ranges, share, half), COLS))
    term = summed(exchange(jnp.broadcast_to(term[None], (chips, share, half)), CHIPS))
    term = exchange(jnp.broadcast_to(term[None], (ranges, share, half)), COLS)
    term = term.reshape(in_width, half)
    weight_grad = joined(term, swap(term)).astype(F32)

    late = swap(jnp.stack([hidden_pair[1], turned[1]]))
    hidden = joined(hidden_pair[0], late[0])
    x_grad = pl.pallas_call(
        feature_kernel,
        out_shape=jax.ShapeDtypeStruct((size, in_width), BF16),
        in_specs=[SMEM, VMEM, VMEM, VMEM],
        out_specs=VMEM,
        compiler_params=params(16),
    )(core, turned[0], late[1], weight)
    return (hidden, x_grad, weight_grad)


def solution(mesh):
    blk, col = mesh.devices.shape
    fine = Mesh(mesh.devices.reshape(blk // 4, 2, 2, 2, col // 2), AXES)
    rows = P(AXES)
    return jax.shard_map(
        per_device,
        mesh=fine,
        in_specs=(rows, rows, P(), rows, rows, rows),
        out_specs=(rows, rows, P()),
        check_vma=False,
    )
```

```python
import functools

import jax
import jax.numpy as jnp
from jax import lax
from jax.experimental import pallas as pl
from jax.experimental.pallas import tpu as pltpu
from jax.sharding import Mesh
from jax.sharding import PartitionSpec as P

AXES = ("y", "xl", "core", "xh", "z")
CHIPS = ("y", "xl")
COLS = ("xh", "z")
SWAP = [(0, 1), (1, 0)]
VMEM = pl.BlockSpec(memory_space=pltpu.VMEM)
SMEM = pl.BlockSpec(memory_space=pltpu.SMEM)
ANY = pl.BlockSpec(memory_space=pl.ANY)
DMA = pltpu.SemaphoreType.DMA
F32 = jnp.float32
BF16 = jnp.bfloat16
SLOTS = 3


def swap(value):
    return lax.ppermute(value, "core", SWAP)


def exchange(value, axes):
    return lax.all_to_all(value, axes, 0, 0, tiled=True)


def copies_kernel(near, far, out):
    for which, half in enumerate((near, far)):
        out[:, which] = jnp.broadcast_to(half[...][None], (out.shape[0],) + half.shape)


def gathered_panels(mine, received, held, first, count):
    shape = (count, 2) + mine.shape

    def gather(near, far):
        copies = pl.pallas_call(
            copies_kernel,
            out_shape=jax.ShapeDtypeStruct(shape, near.dtype),
            in_specs=[VMEM] * 2,
            out_specs=VMEM,
            compiler_params=params(16),
        )(near, far)
        return exchange(copies, "y")

    def skip(near, far):
        return jnp.zeros(shape, near.dtype)

    panels = lax.cond(first, gather, skip, mine, received)
    panels, held = lax.optimization_barrier((panels, held))
    held = lax.ppermute(held, "core", [(0, 1)])
    panels = lax.cond(first, lambda near, far, done: done,
                      lambda near, far, done: gather(near, far), mine, held, panels)
    return panels, lax.ppermute(panels, "xl", SWAP)


def in_hbm(value):
    return pltpu.with_memory_space_constraint(value, pltpu.HBM)


def params(mib):
    return pltpu.CompilerParams(vmem_limit_bytes=mib * 1024 * 1024)


def dot(a, b, contract):
    return lax.dot_general(a, b, (contract, ((), ())), preferred_element_type=F32)


def source_onehot(order):
    size = order.shape[1]
    rows = lax.broadcasted_iota(jnp.int32, (size, size), 0)
    return (rows == order).astype(F32).astype(BF16)


def panel_kernel(ranges, core, order_in, rows_in, features, weight_in, cotangent,
                 mine, near_cot, pack, places, order, rows, weight, sem):
    size, half = mine.shape
    hid = 2 * half
    me = core[0]
    near = pl.ds(pl.multiple_of(me * half, half), half)
    far = pl.ds(pl.multiple_of((1 - me) * half, half), half)
    copies = [
        pltpu.make_async_copy(source, target, sem.at[index])
        for index, (source, target) in enumerate((
            (weight_in, weight),
            (features, pack.at[:size, hid:]),
            (order_in, order),
            (rows_in, rows),
            (cotangent.at[:, near], near_cot),
            (cotangent.at[:, far], pack.at[:size, half:hid]),
        ))
    ]
    for copy in copies:
        copy.start()
    for copy in copies:
        copy.wait()
    whole = dot(pack[:size, hid:], weight[...], ((1,), (0,))).astype(BF16)
    whole = dot(source_onehot(order[...]), whole, ((0,), (0,))).astype(BF16)
    first = me == 0
    left, right = whole[:, :half], whole[:, half:hid]
    mine[...] = jnp.where(first, left, right)
    pack[:size, :half] = jnp.where(first, right, left)
    extra = pack.shape[0] - size
    pack[size:, :] = jnp.zeros((extra, pack.shape[1]), BF16)
    numbers = (extra, size)
    pack[size:, :size] = jnp.broadcast_to(order[...].astype(F32), numbers).astype(BF16)
    ids = rows[:1]
    place = jnp.where(ids >= 0, lax.rem(ids, ranges), ranges)
    places[...] = place
    numbers = (extra, place.shape[1])
    place = jnp.broadcast_to(place.astype(F32), numbers).astype(BF16)
    pack[size:, size:size + place.shape[1]] = place


def multiply(y, column, me, rows_own, rows_other, panels, own, other, total):
    size = own.shape[1]
    for bit in range(2):
        panel = panels[y, bit ^ me]
        base = ((2 * y + column) * 2 + bit) * SLOTS
        here = pl.ds(base, SLOTS)
        ours = dot(own[here].reshape(SLOTS * size, size), panel, ((1,), (0,)))
        theirs = dot(other[here].reshape(SLOTS * size, size), panel, ((1,), (0,)))
        for slot in range(SLOTS):
            take = slice(slot * size, (slot + 1) * size)
            total[0, rows_own[0, base + slot]] += ours[take]
            total[1, rows_other[0, base + slot]] += theirs[take]


def near_kernel(core_x, rows_own, rows_other, panels_in, own_in, other_in,
                total, own, other, panels, sem):
    across = panels.shape[0]
    me, x = core_x[0], core_x[1]
    groups = 2 * SLOTS
    sooner = []
    later = []
    for y in range(across):
        sooner.append(pltpu.make_async_copy(panels_in.at[y], panels.at[y], sem.at[5 * y]))
        for turn, copies in enumerate((sooner, later)):
            column = x if turn == 0 else 1 - x
            tiles = pl.ds((2 * y + column) * groups, groups)
            for which, (source, target) in enumerate(((own_in, own), (other_in, other))):
                copies.append(pltpu.make_async_copy(
                    source.at[tiles], target.at[tiles], sem.at[5 * y + 1 + 2 * turn + which]))
    for copy in sooner + later:
        copy.start()
    total[...] = jnp.zeros_like(total)
    for y in range(across):
        for copy in sooner[3 * y:3 * y + 3]:
            copy.wait()
        multiply(y, x, me, rows_own, rows_other, panels, own, other, total)
    for copy in later:
        copy.wait()


def far_kernel(core_x, rows_own, rows_other, panels, own, other, before, out, total):
    ranges = out.shape[0]
    me, x = core_x[0], core_x[1]
    total[...] = jnp.zeros_like(total)
    for y in range(panels.shape[0]):
        multiply(y, 1 - x, me, rows_own, rows_other, panels, own, other, total)
    for which in range(2):
        out[:, which] = (before[which, :ranges] + total[which, :ranges]).astype(BF16)


def spread_kernel(parts, out):
    total = jnp.sum(parts[...].astype(F32), axis=0).astype(BF16)
    out[...] = jnp.broadcast_to(total[None], out.shape)


def spread(parts, count):
    return pl.pallas_call(
        spread_kernel,
        out_shape=jax.ShapeDtypeStruct((count,) + parts.shape[1:], parts.dtype),
        in_specs=[VMEM],
        out_specs=VMEM,
        compiler_params=params(16),
    )(parts)


def middle_kernel(parts, near_cot, pack, hidden, grad):
    size, half = near_cot.shape
    scale = (2.0 / jnp.pi) ** 0.5
    for which in range(2):
        agg = jnp.sum(parts[:, which].astype(F32), axis=0)
        square = agg * agg
        slope = scale * (1.0 + 3.0 * 0.044715 * square)
        bend = jnp.tanh(scale * (agg + 0.044715 * (agg * square)))
        cdf = 0.5 * (1.0 + bend)
        hidden[which] = (agg * cdf).astype(BF16)
        upstream = near_cot[...] if which == 0 else pack[:size, half:2 * half]
        derivative = cdf + agg * (0.5 * (1.0 - bend * bend) * slope)
        turned = (upstream.astype(F32) * derivative).T.astype(BF16)
        grad[:, which] = jnp.broadcast_to(turned[None], (grad.shape[0],) + turned.shape)


def backward_kernel(core, rows_own, rows_other, grads, own, other, out):
    chips = out.shape[0]
    ranges, _, _, size = grads.shape
    slots = own.shape[0] // (2 * chips)
    me = core[0]
    for group in range(2 * chips):
        lefts = []
        rights = []
        here = slice(group * slots, (group + 1) * slots)
        for which, (tiles, rows) in enumerate(((own, rows_own), (other, rows_other))):
            for slot in range(group * slots, (group + 1) * slots):
                row = rows[0, slot]
                block = grads[jnp.minimum(row, ranges - 1), which]
                lefts.append(jnp.where(row < ranges, block, jnp.zeros_like(block)))
            rights.append(tiles[here].reshape(slots * size, size))
        left = jnp.concatenate(lefts, axis=1)
        right = jnp.concatenate(rights, axis=0)
        out[group // 2, (group % 2) ^ me] = dot(left, right, ((1,), (0,))).astype(BF16)


def weight_kernel(scale, parts, order, features, pack, turned, term):
    size = features.shape[0]
    hid = pack.shape[1] - features.shape[1]
    order_other = pack[size:, :size][:1].astype(F32).astype(jnp.int32)
    both = ((order[...], features[...]), (order_other, pack[:size, hid:]))
    total = 0.0
    for which, (source, values) in enumerate(both):
        panel_grad = jnp.sum(parts[:, which].astype(F32), axis=0).astype(BF16)
        placed = dot(panel_grad, source_onehot(source), ((1,), (1,))).astype(BF16)
        turned[which] = placed
        total = total + dot(placed, values, ((1,), (0,)))
    term[...] = (total * scale).T.astype(BF16)


def feature_kernel(core, mine, theirs, weight, out):
    half = mine.shape[0]
    me = core[0]
    near = weight[:, pl.ds(pl.multiple_of(me * half, half), half)]
    far = weight[:, pl.ds(pl.multiple_of((1 - me) * half, half), half)]
    total = dot(mine[...], near, ((0,), (1,))) + dot(theirs[...], far, ((0,), (1,)))
    out[...] = total.astype(BF16)


def per_device(features, node_order, weight, cotangent, tile_list, tile_values):
    tiles, size, _ = tile_values.shape
    in_width, hid = weight.shape
    half = hid // 2
    chips = lax.axis_size("y") * lax.axis_size("xl")
    ranges = lax.axis_size("xh") * lax.axis_size("z")
    nodes = 2 * chips * ranges * size
    core = lax.axis_index("core").astype(jnp.int32).reshape(1)
    first = core[0] == 0

    def joined(near, far):
        return jnp.where(
            first, jnp.concatenate([near, far], 1), jnp.concatenate([far, near], 1)
        )

    mine, near_cot, pack, rows_own = pl.pallas_call(
        functools.partial(panel_kernel, ranges),
        out_shape=[
            jax.ShapeDtypeStruct((size, half), BF16),
            jax.ShapeDtypeStruct((size, half), BF16),
            jax.ShapeDtypeStruct((size + 16, hid + in_width), BF16),
            jax.ShapeDtypeStruct((1, tiles), jnp.int32),
        ],
        in_specs=[SMEM] + [ANY] * 5,
        out_specs=[VMEM] * 4,
        scratch_shapes=[
            pltpu.VMEM((1, size), jnp.int32),
            pltpu.VMEM((2, tiles), jnp.int32),
            pltpu.VMEM((in_width, hid), BF16),
            DMA((6,)),
        ],
        compiler_params=params(16),
    )(core, *map(in_hbm, (node_order, tile_list.T, features, weight, cotangent)))
    held = pack[:size, :half]
    pack, later_tiles = lax.optimization_barrier((swap(pack), tile_values))
    tiles_other = swap(later_tiles)
    rows_other = pack[size:size + 1, size:size + tiles].astype(jnp.int32)
    across = lax.axis_size("y")
    near, far = gathered_panels(mine, pack[:size, :half], held, first, across)
    core_x = jnp.concatenate([core, lax.axis_index("xl").astype(jnp.int32).reshape(1)])

    total_shape = (2, ranges + 1, size, half)
    half_cost = pl.CostEstimate(
        flops=2 * tiles * size * size * half,
        bytes_accessed=tiles * size * size * 4,
        transcendentals=0,
    )
    partial, tiles_own, tiles_other = pl.pallas_call(
        near_kernel,
        out_shape=[
            jax.ShapeDtypeStruct(total_shape, F32),
            jax.ShapeDtypeStruct(tile_values.shape, BF16),
            jax.ShapeDtypeStruct(tile_values.shape, BF16),
        ],
        in_specs=[SMEM, SMEM, SMEM, ANY, ANY, ANY],
        out_specs=[VMEM] * 3,
        scratch_shapes=[pltpu.VMEM((across, 2, size, half), BF16), DMA((5 * across,))],
        compiler_params=params(24),
        cost_estimate=half_cost,
    )(core_x, rows_own, rows_other, *map(in_hbm, (near, tile_values, tiles_other)))
    partial = pl.pallas_call(
        far_kernel,
        out_shape=jax.ShapeDtypeStruct((ranges, 2, size, half), BF16),
        in_specs=[SMEM, SMEM, SMEM] + [VMEM] * 4,
        out_specs=VMEM,
        scratch_shapes=[pltpu.VMEM(total_shape, F32)],
        compiler_params=params(24),
        cost_estimate=half_cost,
    )(core_x, rows_own, rows_other, far, tiles_own, tiles_other, partial)
    parts = exchange(partial, COLS)
    hidden_pair, grad = pl.pallas_call(
        middle_kernel,
        out_shape=[
            jax.ShapeDtypeStruct((2, size, half), BF16),
            jax.ShapeDtypeStruct((ranges, 2, half, size), BF16),
        ],
        in_specs=[VMEM] * 3,
        out_specs=[VMEM] * 2,
        compiler_params=params(16),
    )(parts, near_cot, pack)
    grads = exchange(grad, COLS)
    contribution = pl.pallas_call(
        backward_kernel,
        out_shape=jax.ShapeDtypeStruct((chips, 2, half, size), BF16),
        in_specs=[SMEM, SMEM, SMEM, VMEM, VMEM, VMEM],
        out_specs=VMEM,
        compiler_params=params(24),
    )(core, rows_own, rows_other, grads, tiles_own, tiles_other)
    parts = exchange(contribution, CHIPS)
    turned, term = pl.pallas_call(
        functools.partial(weight_kernel, nodes ** -0.5),
        out_shape=[
            jax.ShapeDtypeStruct((2, half, size), BF16),
            jax.ShapeDtypeStruct((in_width, half), BF16),
        ],
        in_specs=[VMEM] * 4,
        out_specs=[VMEM] * 2,
        compiler_params=params(16),
    )(parts, node_order, features, pack)

    share = in_width // ranges
    term = exchange(term.reshape(ranges, share, half), COLS)
    term = exchange(spread(term, chips), CHIPS)
    term = exchange(spread(term, ranges), COLS)
    term = term.reshape(in_width, half)
    weight_grad = joined(term, swap(term)).astype(F32)

    late = swap(jnp.stack([hidden_pair[1], turned[1]]))
    hidden = joined(hidden_pair[0], late[0])
    x_grad = pl.pallas_call(
        feature_kernel,
        out_shape=jax.ShapeDtypeStruct((size, in_width), BF16),
        in_specs=[SMEM, VMEM, VMEM, VMEM],
        out_specs=VMEM,
        compiler_params=params(16),
    )(core, turned[0], late[1], weight)
    return (hidden, x_grad, weight_grad)


def solution(mesh):
    blk, col = mesh.devices.shape
    fine = Mesh(mesh.devices.reshape(blk // 4, 2, 2, 2, col // 2), AXES)
    rows = P(AXES)
    return jax.shard_map(
        per_device,
        mesh=fine,
        in_specs=(rows, rows, P(), rows, rows, rows),
        out_specs=(rows, rows, P()),
        check_vma=False,
    )
```

```python
import functools

import jax
import jax.numpy as jnp
from jax import lax
from jax.experimental import pallas as pl
from jax.experimental.pallas import tpu as pltpu
from jax.sharding import Mesh
from jax.sharding import PartitionSpec as P

AXES = ("y", "xl", "core", "xh", "z")
CHIPS = ("y", "xl")
COLS = ("xh", "z")
SWAP = [(0, 1), (1, 0)]
VMEM = pl.BlockSpec(memory_space=pltpu.VMEM)
SMEM = pl.BlockSpec(memory_space=pltpu.SMEM)
ANY = pl.BlockSpec(memory_space=pl.ANY)
DMA = pltpu.SemaphoreType.DMA
F32 = jnp.float32
BF16 = jnp.bfloat16
SLOTS = 3


def swap(value):
    return lax.ppermute(value, "core", SWAP)


def exchange(value, axes):
    return lax.all_to_all(value, axes, 0, 0, tiled=True)


def copies_kernel(near, far, out):
    for which, half in enumerate((near, far)):
        out[:, which] = jnp.broadcast_to(half[...][None], (out.shape[0],) + half.shape)


def copy_kernel(source, target):
    target[...] = source[...]


def copied(value):
    return pl.pallas_call(
        copy_kernel,
        out_shape=pltpu.HBM(value.shape, value.dtype),
        in_specs=[VMEM],
        out_specs=VMEM,
        compiler_params=params(16),
    )(in_hbm(value))


def gathered_panels(mine, received, held, first, count):
    shape = (count, 2) + mine.shape

    def gather(near, far):
        copies = pl.pallas_call(
            copies_kernel,
            out_shape=jax.ShapeDtypeStruct(shape, near.dtype),
            in_specs=[VMEM] * 2,
            out_specs=VMEM,
            compiler_params=params(16),
        )(near, far)
        return exchange(copies, "y")

    def skip(near, far):
        return jnp.zeros(shape, near.dtype)

    panels = lax.cond(first, gather, skip, mine, received)
    panels, held = lax.optimization_barrier((panels, held))
    held = lax.ppermute(held, "core", [(0, 1)])
    panels = lax.cond(first, lambda near, far, done: copied(done),
                      lambda near, far, done: gather(near, far), mine, held, panels)
    return panels, lax.ppermute(panels, "xl", SWAP)


def in_hbm(value):
    return pltpu.with_memory_space_constraint(value, pltpu.HBM)


def params(mib):
    return pltpu.CompilerParams(vmem_limit_bytes=mib * 1024 * 1024)


def dot(a, b, contract):
    return lax.dot_general(a, b, (contract, ((), ())), preferred_element_type=F32)


def source_onehot(order):
    size = order.shape[1]
    rows = lax.broadcasted_iota(jnp.int32, (size, size), 0)
    return (rows == order).astype(F32).astype(BF16)


def panel_kernel(ranges, core, order_in, rows_in, features, weight_in, cotangent,
                 mine, near_cot, pack, places, order, rows, weight, sem):
    size, half = mine.shape
    hid = 2 * half
    me = core[0]
    near = pl.ds(pl.multiple_of(me * half, half), half)
    far = pl.ds(pl.multiple_of((1 - me) * half, half), half)
    copies = [
        pltpu.make_async_copy(source, target, sem.at[index])
        for index, (source, target) in enumerate((
            (weight_in, weight),
            (features, pack.at[:size, hid:]),
            (order_in, order),
            (rows_in, rows),
            (cotangent.at[:, near], near_cot),
            (cotangent.at[:, far], pack.at[:size, half:hid]),
        ))
    ]
    for copy in copies:
        copy.start()
    for copy in copies:
        copy.wait()
    whole = dot(pack[:size, hid:], weight[...], ((1,), (0,))).astype(BF16)
    whole = dot(source_onehot(order[...]), whole, ((0,), (0,))).astype(BF16)
    first = me == 0
    left, right = whole[:, :half], whole[:, half:hid]
    mine[...] = jnp.where(first, left, right)
    pack[:size, :half] = jnp.where(first, right, left)
    extra = pack.shape[0] - size
    pack[size:, :] = jnp.zeros((extra, pack.shape[1]), BF16)
    numbers = (extra, size)
    pack[size:, :size] = jnp.broadcast_to(order[...].astype(F32), numbers).astype(BF16)
    ids = rows[:1]
    place = jnp.where(ids >= 0, lax.rem(ids, ranges), ranges)
    places[...] = place
    numbers = (extra, place.shape[1])
    place = jnp.broadcast_to(place.astype(F32), numbers).astype(BF16)
    pack[size:, size:size + place.shape[1]] = place


def multiply(y, column, me, rows_own, rows_other, panels, own, other, total):
    size = own.shape[1]
    for bit in range(2):
        panel = panels[y, bit ^ me]
        base = ((2 * y + column) * 2 + bit) * SLOTS
        here = pl.ds(base, SLOTS)
        ours = dot(own[here].reshape(SLOTS * size, size), panel, ((1,), (0,)))
        theirs = dot(other[here].reshape(SLOTS * size, size), panel, ((1,), (0,)))
        for slot in range(SLOTS):
            take = slice(slot * size, (slot + 1) * size)
            total[0, rows_own[0, base + slot]] += ours[take]
            total[1, rows_other[0, base + slot]] += theirs[take]


def near_kernel(core_x, rows_own, rows_other, panels_in, own_in, other_in,
                total, own, other, panels, sem):
    across = panels.shape[0]
    me, x = core_x[0], core_x[1]
    groups = 2 * SLOTS
    sooner = []
    later = []
    for y in range(across):
        sooner.append(pltpu.make_async_copy(panels_in.at[y], panels.at[y], sem.at[5 * y]))
        for turn, copies in enumerate((sooner, later)):
            column = x if turn == 0 else 1 - x
            tiles = pl.ds((2 * y + column) * groups, groups)
            for which, (source, target) in enumerate(((own_in, own), (other_in, other))):
                copies.append(pltpu.make_async_copy(
                    source.at[tiles], target.at[tiles], sem.at[5 * y + 1 + 2 * turn + which]))
    for copy in sooner + later:
        copy.start()
    total[...] = jnp.zeros_like(total)
    for y in range(across):
        for copy in sooner[3 * y:3 * y + 3]:
            copy.wait()
        multiply(y, x, me, rows_own, rows_other, panels, own, other, total)
    for copy in later:
        copy.wait()


def far_kernel(core_x, rows_own, rows_other, panels, own, other, before, out, total):
    ranges = out.shape[0]
    me, x = core_x[0], core_x[1]
    total[...] = jnp.zeros_like(total)
    for y in range(panels.shape[0]):
        multiply(y, 1 - x, me, rows_own, rows_other, panels, own, other, total)
    for which in range(2):
        out[:, which] = (before[which, :ranges] + total[which, :ranges]).astype(BF16)


def spread_kernel(parts, out):
    total = jnp.sum(parts[...].astype(F32), axis=0).astype(BF16)
    out[...] = jnp.broadcast_to(total[None], out.shape)


def spread(parts, count):
    return pl.pallas_call(
        spread_kernel,
        out_shape=jax.ShapeDtypeStruct((count,) + parts.shape[1:], parts.dtype),
        in_specs=[VMEM],
        out_specs=VMEM,
        compiler_params=params(16),
    )(parts)


def middle_kernel(parts, near_cot, pack, hidden, grad):
    size, half = near_cot.shape
    scale = (2.0 / jnp.pi) ** 0.5
    for which in range(2):
        agg = jnp.sum(parts[:, which].astype(F32), axis=0)
        square = agg * agg
        slope = scale * (1.0 + 3.0 * 0.044715 * square)
        bend = jnp.tanh(scale * (agg + 0.044715 * (agg * square)))
        cdf = 0.5 * (1.0 + bend)
        hidden[which] = (agg * cdf).astype(BF16)
        upstream = near_cot[...] if which == 0 else pack[:size, half:2 * half]
        derivative = cdf + agg * (0.5 * (1.0 - bend * bend) * slope)
        turned = (upstream.astype(F32) * derivative).T.astype(BF16)
        grad[:, which] = jnp.broadcast_to(turned[None], (grad.shape[0],) + turned.shape)


def backward_kernel(core, rows_own, rows_other, grads, own, other, out):
    chips = out.shape[0]
    ranges, _, _, size = grads.shape
    slots = own.shape[0] // (2 * chips)
    me = core[0]
    for group in range(2 * chips):
        lefts = []
        rights = []
        here = slice(group * slots, (group + 1) * slots)
        for which, (tiles, rows) in enumerate(((own, rows_own), (other, rows_other))):
            for slot in range(group * slots, (group + 1) * slots):
                row = rows[0, slot]
                block = grads[jnp.minimum(row, ranges - 1), which]
                lefts.append(jnp.where(row < ranges, block, jnp.zeros_like(block)))
            rights.append(tiles[here].reshape(slots * size, size))
        left = jnp.concatenate(lefts, axis=1)
        right = jnp.concatenate(rights, axis=0)
        out[group // 2, (group % 2) ^ me] = dot(left, right, ((1,), (0,))).astype(BF16)


def weight_kernel(scale, parts, order, features, pack, turned, term):
    size = features.shape[0]
    hid = pack.shape[1] - features.shape[1]
    order_other = pack[size:, :size][:1].astype(F32).astype(jnp.int32)
    both = ((order[...], features[...]), (order_other, pack[:size, hid:]))
    total = 0.0
    for which, (source, values) in enumerate(both):
        panel_grad = jnp.sum(parts[:, which].astype(F32), axis=0).astype(BF16)
        placed = dot(panel_grad, source_onehot(source), ((1,), (1,))).astype(BF16)
        turned[which] = placed
        total = total + dot(placed, values, ((1,), (0,)))
    term[...] = (total * scale).T.astype(BF16)


def feature_kernel(core, mine, theirs, weight, out):
    half = mine.shape[0]
    me = core[0]
    near = weight[:, pl.ds(pl.multiple_of(me * half, half), half)]
    far = weight[:, pl.ds(pl.multiple_of((1 - me) * half, half), half)]
    total = dot(mine[...], near, ((0,), (1,))) + dot(theirs[...], far, ((0,), (1,)))
    out[...] = total.astype(BF16)


def per_device(features, node_order, weight, cotangent, tile_list, tile_values):
    tiles, size, _ = tile_values.shape
    in_width, hid = weight.shape
    half = hid // 2
    chips = lax.axis_size("y") * lax.axis_size("xl")
    ranges = lax.axis_size("xh") * lax.axis_size("z")
    nodes = 2 * chips * ranges * size
    core = lax.axis_index("core").astype(jnp.int32).reshape(1)
    first = core[0] == 0

    def joined(near, far):
        return jnp.where(
            first, jnp.concatenate([near, far], 1), jnp.concatenate([far, near], 1)
        )

    mine, near_cot, pack, rows_own = pl.pallas_call(
        functools.partial(panel_kernel, ranges),
        out_shape=[
            jax.ShapeDtypeStruct((size, half), BF16),
            jax.ShapeDtypeStruct((size, half), BF16),
            jax.ShapeDtypeStruct((size + 16, hid + in_width), BF16),
            jax.ShapeDtypeStruct((1, tiles), jnp.int32),
        ],
        in_specs=[SMEM] + [ANY] * 5,
        out_specs=[VMEM] * 4,
        scratch_shapes=[
            pltpu.VMEM((1, size), jnp.int32),
            pltpu.VMEM((2, tiles), jnp.int32),
            pltpu.VMEM((in_width, hid), BF16),
            DMA((6,)),
        ],
        compiler_params=params(16),
    )(core, *map(in_hbm, (node_order, tile_list.T, features, weight, cotangent)))
    held = pack[:size, :half]
    pack, later_tiles = lax.optimization_barrier((swap(pack), tile_values))
    tiles_other = swap(later_tiles)
    rows_other = pack[size:size + 1, size:size + tiles].astype(jnp.int32)
    across = lax.axis_size("y")
    near, far = gathered_panels(mine, pack[:size, :half], held, first, across)
    core_x = jnp.concatenate([core, lax.axis_index("xl").astype(jnp.int32).reshape(1)])

    total_shape = (2, ranges + 1, size, half)
    half_cost = pl.CostEstimate(
        flops=2 * tiles * size * size * half,
        bytes_accessed=tiles * size * size * 4,
        transcendentals=0,
    )
    partial, tiles_own, tiles_other = pl.pallas_call(
        near_kernel,
        out_shape=[
            jax.ShapeDtypeStruct(total_shape, F32),
            jax.ShapeDtypeStruct(tile_values.shape, BF16),
            jax.ShapeDtypeStruct(tile_values.shape, BF16),
        ],
        in_specs=[SMEM, SMEM, SMEM, ANY, ANY, ANY],
        out_specs=[VMEM] * 3,
        scratch_shapes=[pltpu.VMEM((across, 2, size, half), BF16), DMA((5 * across,))],
        compiler_params=params(24),
        cost_estimate=half_cost,
    )(core_x, rows_own, rows_other, *map(in_hbm, (near, tile_values, tiles_other)))
    partial = pl.pallas_call(
        far_kernel,
        out_shape=jax.ShapeDtypeStruct((ranges, 2, size, half), BF16),
        in_specs=[SMEM, SMEM, SMEM] + [VMEM] * 4,
        out_specs=VMEM,
        scratch_shapes=[pltpu.VMEM(total_shape, F32)],
        compiler_params=params(24),
        cost_estimate=half_cost,
    )(core_x, rows_own, rows_other, far, tiles_own, tiles_other, partial)
    parts = exchange(partial, COLS)
    hidden_pair, grad = pl.pallas_call(
        middle_kernel,
        out_shape=[
            jax.ShapeDtypeStruct((2, size, half), BF16),
            jax.ShapeDtypeStruct((ranges, 2, half, size), BF16),
        ],
        in_specs=[VMEM] * 3,
        out_specs=[VMEM] * 2,
        compiler_params=params(16),
    )(parts, near_cot, pack)
    grads = exchange(grad, COLS)
    contribution = pl.pallas_call(
        backward_kernel,
        out_shape=jax.ShapeDtypeStruct((chips, 2, half, size), BF16),
        in_specs=[SMEM, SMEM, SMEM, VMEM, VMEM, VMEM],
        out_specs=VMEM,
        compiler_params=params(24),
    )(core, rows_own, rows_other, grads, tiles_own, tiles_other)
    parts = exchange(contribution, CHIPS)
    turned, term = pl.pallas_call(
        functools.partial(weight_kernel, nodes ** -0.5),
        out_shape=[
            jax.ShapeDtypeStruct((2, half, size), BF16),
            jax.ShapeDtypeStruct((in_width, half), BF16),
        ],
        in_specs=[VMEM] * 4,
        out_specs=[VMEM] * 2,
        compiler_params=params(16),
    )(parts, node_order, features, pack)

    share = in_width // ranges
    term = exchange(term.reshape(ranges, share, half), COLS)
    term = exchange(spread(term, chips), CHIPS)
    term = exchange(spread(term, ranges), COLS)
    term = term.reshape(in_width, half)
    weight_grad = joined(term, swap(term)).astype(F32)

    late = swap(jnp.stack([hidden_pair[1], turned[1]]))
    hidden = joined(hidden_pair[0], late[0])
    x_grad = pl.pallas_call(
        feature_kernel,
        out_shape=jax.ShapeDtypeStruct((size, in_width), BF16),
        in_specs=[SMEM, VMEM, VMEM, VMEM],
        out_specs=VMEM,
        compiler_params=params(16),
    )(core, turned[0], late[1], weight)
    return (hidden, x_grad, weight_grad)


def solution(mesh):
    blk, col = mesh.devices.shape
    fine = Mesh(mesh.devices.reshape(blk // 4, 2, 2, 2, col // 2), AXES)
    rows = P(AXES)
    return jax.shard_map(
        per_device,
        mesh=fine,
        in_specs=(rows, rows, P(), rows, rows, rows),
        out_specs=(rows, rows, P()),
        check_vma=False,
    )
```

```python
import functools

import jax
import jax.numpy as jnp
from jax import lax
from jax.experimental import pallas as pl
from jax.experimental.pallas import tpu as pltpu
from jax.sharding import Mesh
from jax.sharding import PartitionSpec as P

AXES = ("y", "xl", "core", "xh", "z")
CHIPS = ("y", "xl")
COLS = ("xh", "z")
SWAP = [(0, 1), (1, 0)]
VMEM = pl.BlockSpec(memory_space=pltpu.VMEM)
SMEM = pl.BlockSpec(memory_space=pltpu.SMEM)
ANY = pl.BlockSpec(memory_space=pl.ANY)
DMA = pltpu.SemaphoreType.DMA
F32 = jnp.float32
BF16 = jnp.bfloat16
SLOTS = 3


def swap(value):
    return lax.ppermute(value, "core", SWAP)


def exchange(value, axes):
    return lax.all_to_all(value, axes, 0, 0, tiled=True)


def copies_kernel(near, far, out):
    for which, half in enumerate((near, far)):
        out[:, which] = jnp.broadcast_to(half[...][None], (out.shape[0],) + half.shape)


def copy_kernel(source, target):
    target[...] = source[...]


def copied(value):
    return pl.pallas_call(
        copy_kernel,
        out_shape=pltpu.HBM(value.shape, value.dtype),
        in_specs=[VMEM],
        out_specs=VMEM,
        compiler_params=params(16),
    )(in_hbm(value))


def gathered_panels(mine, received, held, first, count):
    shape = (count, 2) + mine.shape

    def gather(near, far):
        copies = pl.pallas_call(
            copies_kernel,
            out_shape=jax.ShapeDtypeStruct(shape, near.dtype),
            in_specs=[VMEM] * 2,
            out_specs=VMEM,
            compiler_params=params(16),
        )(near, far)
        return exchange(copies, "y")

    def skip(near, far):
        return jnp.zeros(shape, near.dtype)

    panels = lax.cond(first, gather, skip, mine, received)
    panels, held = lax.optimization_barrier((panels, held))
    held = lax.ppermute(held, "core", [(0, 1)])
    panels = lax.cond(first, lambda near, far, done: copied(done),
                      lambda near, far, done: gather(near, far), mine, held, panels)
    return panels, lax.ppermute(panels, "xl", SWAP)


def in_hbm(value):
    return pltpu.with_memory_space_constraint(value, pltpu.HBM)


def params(mib):
    return pltpu.CompilerParams(vmem_limit_bytes=mib * 1024 * 1024)


def dot(a, b, contract):
    return lax.dot_general(a, b, (contract, ((), ())), preferred_element_type=F32)


def source_onehot(order):
    size = order.shape[1]
    rows = lax.broadcasted_iota(jnp.int32, (size, size), 0)
    return (rows == order).astype(F32).astype(BF16)


def panel_kernel(ranges, core, order_in, rows_in, features, weight_in, cotangent,
                 mine, near_cot, pack, places, order, rows, weight, sem):
    size, half = mine.shape
    hid = 2 * half
    me = core[0]
    near = pl.ds(pl.multiple_of(me * half, half), half)
    far = pl.ds(pl.multiple_of((1 - me) * half, half), half)
    copies = [
        pltpu.make_async_copy(source, target, sem.at[index])
        for index, (source, target) in enumerate((
            (weight_in, weight),
            (features, pack.at[:size, hid:]),
            (order_in, order),
            (rows_in, rows),
            (cotangent.at[:, near], near_cot),
            (cotangent.at[:, far], pack.at[:size, half:hid]),
        ))
    ]
    for copy in copies:
        copy.start()
    for copy in copies:
        copy.wait()
    whole = dot(pack[:size, hid:], weight[...], ((1,), (0,))).astype(BF16)
    whole = dot(source_onehot(order[...]), whole, ((0,), (0,))).astype(BF16)
    first = me == 0
    left, right = whole[:, :half], whole[:, half:hid]
    mine[...] = jnp.where(first, left, right)
    pack[:size, :half] = jnp.where(first, right, left)
    extra = pack.shape[0] - size
    pack[size:, :] = jnp.zeros((extra, pack.shape[1]), BF16)
    numbers = (extra, size)
    pack[size:, :size] = jnp.broadcast_to(order[...].astype(F32), numbers).astype(BF16)
    ids = rows[:1]
    place = jnp.where(ids >= 0, lax.rem(ids, ranges), ranges)
    places[...] = place
    numbers = (extra, place.shape[1])
    place = jnp.broadcast_to(place.astype(F32), numbers).astype(BF16)
    pack[size:, size:size + place.shape[1]] = place


def multiply(y, column, me, rows_own, rows_other, panels, own, other, total):
    size = own.shape[1]
    for bit in range(2):
        panel = panels[y, bit ^ me]
        base = ((2 * y + column) * 2 + bit) * SLOTS
        here = pl.ds(base, SLOTS)
        ours = dot(own[here].reshape(SLOTS * size, size), panel, ((1,), (0,)))
        theirs = dot(other[here].reshape(SLOTS * size, size), panel, ((1,), (0,)))
        for slot in range(SLOTS):
            take = slice(slot * size, (slot + 1) * size)
            total[0, rows_own[0, base + slot]] += ours[take]
            total[1, rows_other[0, base + slot]] += theirs[take]


def near_kernel(core_x, rows_own, rows_other, panels_in, own_in, other_in,
                total, own, other, panels, sem):
    across = panels.shape[0]
    me, x = core_x[0], core_x[1]
    groups = 2 * SLOTS
    sooner = []
    later = []
    for y in range(across):
        sooner.append(pltpu.make_async_copy(panels_in.at[y], panels.at[y], sem.at[5 * y]))
        for turn, copies in enumerate((sooner, later)):
            column = x if turn == 0 else 1 - x
            tiles = pl.ds((2 * y + column) * groups, groups)
            for which, (source, target) in enumerate(((own_in, own), (other_in, other))):
                copies.append(pltpu.make_async_copy(
                    source.at[tiles], target.at[tiles], sem.at[5 * y + 1 + 2 * turn + which]))
    for copy in sooner + later:
        copy.start()
    total[...] = jnp.zeros_like(total)
    for y in range(across):
        for copy in sooner[3 * y:3 * y + 3]:
            copy.wait()
        multiply(y, x, me, rows_own, rows_other, panels, own, other, total)
    for copy in later:
        copy.wait()


def far_kernel(core_x, rows_own, rows_other, panels, own, other, before, out, total):
    ranges = out.shape[0]
    me, x = core_x[0], core_x[1]
    total[...] = jnp.zeros_like(total)
    for y in range(panels.shape[0]):
        multiply(y, 1 - x, me, rows_own, rows_other, panels, own, other, total)
    for which in range(2):
        out[:, which] = (before[which, :ranges] + total[which, :ranges]).astype(BF16)


def spread_kernel(parts, out):
    total = jnp.sum(parts[...].astype(F32), axis=0).astype(BF16)
    out[...] = jnp.broadcast_to(total[None], out.shape)


def spread(parts, count):
    return pl.pallas_call(
        spread_kernel,
        out_shape=jax.ShapeDtypeStruct((count,) + parts.shape[1:], parts.dtype),
        in_specs=[VMEM],
        out_specs=VMEM,
        compiler_params=params(16),
    )(parts)


def middle_kernel(parts, near_cot, pack, hidden, grad):
    size, half = near_cot.shape
    scale = (2.0 / jnp.pi) ** 0.5
    for which in range(2):
        agg = jnp.sum(parts[:, which].astype(F32), axis=0)
        square = agg * agg
        slope = scale * (1.0 + 3.0 * 0.044715 * square)
        bend = jnp.tanh(scale * (agg + 0.044715 * (agg * square)))
        cdf = 0.5 * (1.0 + bend)
        hidden[which] = (agg * cdf).astype(BF16)
        upstream = near_cot[...] if which == 0 else pack[:size, half:2 * half]
        derivative = cdf + agg * (0.5 * (1.0 - bend * bend) * slope)
        turned = (upstream.astype(F32) * derivative).T.astype(BF16)
        grad[:, which] = jnp.broadcast_to(turned[None], (grad.shape[0],) + turned.shape)


def backward_kernel(core, rows_own, rows_other, grads, own, other, out):
    chips = out.shape[0]
    ranges, _, _, size = grads.shape
    slots = own.shape[0] // (2 * chips)
    me = core[0]
    for group in range(2 * chips):
        lefts = []
        rights = []
        here = slice(group * slots, (group + 1) * slots)
        for which, (tiles, rows) in enumerate(((own, rows_own), (other, rows_other))):
            for slot in range(group * slots, (group + 1) * slots):
                row = rows[0, slot]
                block = grads[jnp.minimum(row, ranges - 1), which]
                lefts.append(jnp.where(row < ranges, block, jnp.zeros_like(block)))
            rights.append(tiles[here].reshape(slots * size, size))
        left = jnp.concatenate(lefts, axis=1)
        right = jnp.concatenate(rights, axis=0)
        out[group // 2, (group % 2) ^ me] = dot(left, right, ((1,), (0,))).astype(BF16)


def weight_kernel(scale, parts, order, features, pack, hidden, turned, late, term):
    size = features.shape[0]
    hid = pack.shape[1] - features.shape[1]
    order_other = pack[size:, :size][:1].astype(F32).astype(jnp.int32)
    both = ((order[...], features[...]), (order_other, pack[:size, hid:]))
    total = 0.0
    for which, (source, values) in enumerate(both):
        panel_grad = jnp.sum(parts[:, which].astype(F32), axis=0).astype(BF16)
        placed = dot(panel_grad, source_onehot(source), ((1,), (1,))).astype(BF16)
        if which == 0:
            turned[...] = placed
        else:
            late[1] = placed
        total = total + dot(placed, values, ((1,), (0,)))
    late[0] = hidden[1]
    term[...] = (total * scale).T.astype(BF16)


def feature_kernel(core, mine, late, hidden_pair, weight, out, hidden):
    half = mine.shape[0]
    me = core[0]
    near = pl.ds(pl.multiple_of(me * half, half), half)
    far = pl.ds(pl.multiple_of((1 - me) * half, half), half)
    total = dot(mine[...], weight[:, near], ((0,), (1,)))
    total = total + dot(late[1], weight[:, far], ((0,), (1,)))
    out[...] = total.astype(BF16)
    hidden[:, near] = hidden_pair[0]
    hidden[:, far] = late[0]


def per_device(features, node_order, weight, cotangent, tile_list, tile_values):
    tiles, size, _ = tile_values.shape
    in_width, hid = weight.shape
    half = hid // 2
    chips = lax.axis_size("y") * lax.axis_size("xl")
    ranges = lax.axis_size("xh") * lax.axis_size("z")
    nodes = 2 * chips * ranges * size
    core = lax.axis_index("core").astype(jnp.int32).reshape(1)
    first = core[0] == 0

    def joined(near, far):
        return jnp.where(
            first, jnp.concatenate([near, far], 1), jnp.concatenate([far, near], 1)
        )

    mine, near_cot, pack, rows_own = pl.pallas_call(
        functools.partial(panel_kernel, ranges),
        out_shape=[
            jax.ShapeDtypeStruct((size, half), BF16),
            jax.ShapeDtypeStruct((size, half), BF16),
            jax.ShapeDtypeStruct((size + 16, hid + in_width), BF16),
            jax.ShapeDtypeStruct((1, tiles), jnp.int32),
        ],
        in_specs=[SMEM] + [ANY] * 5,
        out_specs=[VMEM] * 4,
        scratch_shapes=[
            pltpu.VMEM((1, size), jnp.int32),
            pltpu.VMEM((2, tiles), jnp.int32),
            pltpu.VMEM((in_width, hid), BF16),
            DMA((6,)),
        ],
        compiler_params=params(16),
    )(core, *map(in_hbm, (node_order, tile_list.T, features, weight, cotangent)))
    held = pack[:size, :half]
    pack, later_tiles = lax.optimization_barrier((swap(pack), tile_values))
    tiles_other = swap(later_tiles)
    rows_other = pack[size:size + 1, size:size + tiles].astype(jnp.int32)
    across = lax.axis_size("y")
    near, far = gathered_panels(mine, pack[:size, :half], held, first, across)
    core_x = jnp.concatenate([core, lax.axis_index("xl").astype(jnp.int32).reshape(1)])

    total_shape = (2, ranges + 1, size, half)
    half_cost = pl.CostEstimate(
        flops=2 * tiles * size * size * half,
        bytes_accessed=tiles * size * size * 4,
        transcendentals=0,
    )
    partial, tiles_own, tiles_other = pl.pallas_call(
        near_kernel,
        out_shape=[
            jax.ShapeDtypeStruct(total_shape, F32),
            jax.ShapeDtypeStruct(tile_values.shape, BF16),
            jax.ShapeDtypeStruct(tile_values.shape, BF16),
        ],
        in_specs=[SMEM, SMEM, SMEM, ANY, ANY, ANY],
        out_specs=[VMEM] * 3,
        scratch_shapes=[pltpu.VMEM((across, 2, size, half), BF16), DMA((5 * across,))],
        compiler_params=params(24),
        cost_estimate=half_cost,
    )(core_x, rows_own, rows_other, *map(in_hbm, (near, tile_values, tiles_other)))
    partial = pl.pallas_call(
        far_kernel,
        out_shape=jax.ShapeDtypeStruct((ranges, 2, size, half), BF16),
        in_specs=[SMEM, SMEM, SMEM] + [VMEM] * 4,
        out_specs=VMEM,
        scratch_shapes=[pltpu.VMEM(total_shape, F32)],
        compiler_params=params(24),
        cost_estimate=half_cost,
    )(core_x, rows_own, rows_other, far, tiles_own, tiles_other, partial)
    parts = exchange(partial, COLS)
    hidden_pair, grad = pl.pallas_call(
        middle_kernel,
        out_shape=[
            jax.ShapeDtypeStruct((2, size, half), BF16),
            jax.ShapeDtypeStruct((ranges, 2, half, size), BF16),
        ],
        in_specs=[VMEM] * 3,
        out_specs=[VMEM] * 2,
        compiler_params=params(16),
    )(parts, near_cot, pack)
    grads = exchange(grad, COLS)
    contribution = pl.pallas_call(
        backward_kernel,
        out_shape=jax.ShapeDtypeStruct((chips, 2, half, size), BF16),
        in_specs=[SMEM, SMEM, SMEM, VMEM, VMEM, VMEM],
        out_specs=VMEM,
        compiler_params=params(24),
    )(core, rows_own, rows_other, grads, tiles_own, tiles_other)
    parts = exchange(contribution, CHIPS)
    turned, late, term = pl.pallas_call(
        functools.partial(weight_kernel, nodes ** -0.5),
        out_shape=[
            jax.ShapeDtypeStruct((half, size), BF16),
            jax.ShapeDtypeStruct((2, size, half), BF16),
            jax.ShapeDtypeStruct((in_width, half), BF16),
        ],
        in_specs=[VMEM] * 5,
        out_specs=[VMEM] * 3,
        compiler_params=params(16),
    )(parts, node_order, features, pack, hidden_pair)

    share = in_width // ranges
    term = exchange(term.reshape(ranges, share, half), COLS)
    term = exchange(spread(term, chips), CHIPS)
    term = exchange(spread(term, ranges), COLS)
    term = term.reshape(in_width, half)
    weight_grad = joined(term, swap(term)).astype(F32)

    x_grad, hidden = pl.pallas_call(
        feature_kernel,
        out_shape=[
            jax.ShapeDtypeStruct((size, in_width), BF16),
            jax.ShapeDtypeStruct((size, hid), BF16),
        ],
        in_specs=[SMEM, VMEM, VMEM, VMEM, VMEM],
        out_specs=[VMEM] * 2,
        compiler_params=params(16),
    )(core, turned, swap(late), hidden_pair, weight)
    return (hidden, x_grad, weight_grad)


def solution(mesh):
    blk, col = mesh.devices.shape
    fine = Mesh(mesh.devices.reshape(blk // 4, 2, 2, 2, col // 2), AXES)
    rows = P(AXES)
    return jax.shard_map(
        per_device,
        mesh=fine,
        in_specs=(rows, rows, P(), rows, rows, rows),
        out_specs=(rows, rows, P()),
        check_vma=False,
    )
```
